32 devices in a mesh: groups: 2 (over y), dom: 16 (over z, x, core).
Axes of the slice: x: 2, y: 2, z: 4, core: 2. Of those that a mesh axis runs over, the one named last changes fastest.
Arguments:
- nodes: float32 [65536, 128], P(('groups', 'dom')), parts along dimension 0, may hold values from -6 to 6
- edges: float32 [512, 4, 128], P(('groups', 'dom')), parts along dimension 0, may hold values from -6 to 6
- adjacency: int32 [512, 4], P(('groups', 'dom')), parts along dimension 0, may hold values from 0 to 19
- boundary: int32 [64, 2], P(('groups', 'dom')), parts along dimension 0, may hold values from 0 to 15
- assign: int32 [65536], P(('groups', 'dom')), parts along dimension 0, may hold values from 0 to 767
- coarse_adj: int32 [64, 4], P(('groups', 'dom')), parts along dimension 0, may hold values from 0 to 5
- coarse_edges: float32 [64, 4, 128], P(('groups', 'dom')), parts along dimension 0, may hold values from -6 to 6
- counts: int32 [32], P(('groups', 'dom')), parts along dimension 0, may hold values from 8 to 16
- targets: float32 [4, 65536], P(None, ('groups', 'dom')), parts along dimension 1, may hold values from -6 to 6
- w_send: float32 [3, 128, 128], replicated, may hold values from -0.5 to 0.5
- w_recv: float32 [3, 128, 128], replicated, may hold values from -0.5 to 0.5
- w_update: float32 [3, 128, 128], replicated, may hold values from -0.5 to 0.5
- w_edge: float32 [3, 128], replicated, may hold values from -6 to 6
- bias: float32 [3, 128], replicated, may hold values from -3 to 3
- w_out: float32 [4, 128], replicated, may hold values from -0.5 to 0.5
Outputs:
- loss: float32 [2], P('groups'), parts along dimension 0
- d_nodes: float32 [65536, 128], P(('groups', 'dom')), parts along dimension 0
- g_send: float32 [6, 128, 128], P('groups'), parts along dimension 0
- g_recv: float32 [6, 128, 128], P('groups'), parts along dimension 0
- g_update: float32 [6, 128, 128], P('groups'), parts along dimension 0
- g_edge: float32 [6, 128], P('groups'), parts along dimension 0
- g_bias: float32 [6, 128], P('groups'), parts along dimension 0
- g_out: float32 [8, 128], P('groups'), parts along dimension 0
The draws below stay inside these ranges and needn't reach their ends.
There are 2 independent parts, one for each index of `groups`. The reference program is written for one: setup_inputs(seed, part) draws one part's arguments, and reference() takes and returns one part's arrays. A program takes and returns all parts, laid end to end along the dimension named above; an argument that names none is the same for every part. Nothing has to cross between parts.
Inputs may be any that keep to these rules, and one draw needn't show every extreme that they name: `adjacency`: indices into own blocks (16), then 2 from the lower partition, then 2 from the upper. `boundary`: local block indices.
All inputs are finite; a program needn't handle non-finite values.
Results may differ from the reference program's by a relative error of at most 0.0003.
Values sent between devices are 32-bit elements; how exact they have to be, the bound alone decides.
A program may use at most 128 MiB of HBM per device.

```python
import jax
import jax.numpy as jnp
from jax import lax

H = 128
B = 128
NBD = 16
K = 4
KC = 4
NH = 2
NCB = 2
NCD = 256
BLOCKS = 256
CBLOCKS = 32
NODES = 32768
N_DOM = 16


def plant(entries, rng, smallest, high):
    index_at = [jax.random.randint(jax.random.fold_in(rng, axis), (), 0, length) for axis, length in enumerate(entries.shape)]
    main_axis = entries.shape.index(max(entries.shape))
    next_to = index_at[:main_axis] + [(index_at[main_axis] + 1) % entries.shape[main_axis]] + index_at[main_axis + 1:]
    return entries.at[tuple(index_at)].set(smallest).at[tuple(next_to)].set(high)


def block_levels(own_key, dims, split, least, top_value):
    gain = 1.0
    for axis_at, blocks in split:
        steps = jax.random.uniform(jax.random.fold_in(jax.random.fold_in(own_key, 6), axis_at), (blocks,), jnp.float32, least / len(split), top_value / len(split))
        gain = gain * jnp.repeat(jnp.exp(steps), dims[axis_at] // blocks).reshape((-1,) + (1,) * (len(dims) - 1 - axis_at))
    return gain


def noise(own_key, shape, spread, limit, shards=(), kind=jnp.bfloat16):
    factor_of = block_levels(own_key, shape, shards, -0.22, 0.18) if shards else 1.0
    array = jax.random.normal(own_key, shape, jnp.float32) * spread * factor_of
    return jnp.minimum(jnp.maximum(array, -limit), limit).astype(kind)


def setup_inputs(seed: int = 0, part: int = 0) -> dict:
    arg_keys = jax.random.split(jax.random.key(seed), 16)
    part_keys = jax.random.split(jax.random.fold_in(arg_keys[15], part), 16)
    return {
        "nodes": noise(part_keys[0], (NODES, H), 1.0, 6.0, ((0, 16),), jnp.float32),
        "edges": noise(part_keys[1], (BLOCKS, K, B), 1.0, 6.0, ((0, 16),), jnp.float32),
        "adjacency": plant(jax.random.randint(part_keys[2], (BLOCKS, K), 0, NBD + 2 * NH), jax.random.fold_in(part_keys[2], 1), 0, (NBD + 2 * NH) - 1).astype(jnp.int32),
        "boundary": plant(jax.random.randint(part_keys[3], (2 * N_DOM, NH), 0, NBD), jax.random.fold_in(part_keys[3], 1), 0, NBD - 1).astype(jnp.int32),
        "assign": plant(jax.random.randint(part_keys[4], (NODES,), 0, 3 * NCD), jax.random.fold_in(part_keys[4], 1), 0, (3 * NCD) - 1).astype(jnp.int32),
        "coarse_adj": plant(jax.random.randint(part_keys[5], (CBLOCKS, KC), 0, 3 * NCB), jax.random.fold_in(part_keys[5], 1), 0, (3 * NCB) - 1).astype(jnp.int32),
        "coarse_edges": noise(part_keys[6], (CBLOCKS, KC, B), 1.0, 6.0, ((0, 16),), jnp.float32),
        "counts": plant(jax.random.randint(part_keys[7], (N_DOM,), NBD // 2, NBD + 1), jax.random.fold_in(part_keys[7], 1), NBD // 2, NBD).astype(jnp.int32),
        "targets": noise(part_keys[8], (4, NODES), 1.0, 6.0, ((1, 16),), jnp.float32),
        "w_send": noise(arg_keys[9], (3, H, H), H ** -0.5, 0.5, (), jnp.float32),
        "w_recv": noise(arg_keys[10], (3, H, H), H ** -0.5, 0.5, (), jnp.float32),
        "w_update": noise(arg_keys[11], (3, H, H), H ** -0.5, 0.5, (), jnp.float32),
        "w_edge": noise(arg_keys[12], (3, H), 1.0, 6.0, (), jnp.float32),
        "bias": noise(arg_keys[13], (3, H), 0.5, 3.0, (), jnp.float32),
        "w_out": noise(arg_keys[14], (4, H), H ** -0.5, 0.5, (), jnp.float32),
    }


HIGH = lax.Precision.HIGHEST

def shift_dev(values, offset):
    zero = jnp.zeros_like(values[:1])
    if offset > 0:
        return jnp.concatenate([zero, values[:-1]], 0)
    return jnp.concatenate([values[1:], zero], 0)

def pick_rows(values, index):
    return jax.vmap(lambda table, rows: table[rows])(values, index)

def layer(feats, adj, edge, out_up, out_down, w_s, w_r, w_u, w_e, b_l, mask):
    ext = jnp.concatenate([feats, shift_dev(out_up, 1), shift_dev(out_down, -1)], 1)
    neigh = pick_rows(ext, adj)
    own = jnp.einsum('pnbh,hg->pnbg', feats, w_s, precision=HIGH)
    pre = own[:, :, None] + jnp.einsum('pnkbh,hg->pnkbg', neigh, w_r, precision=HIGH) + edge[..., None] * w_e + b_l
    agg = lax.optimization_barrier(jnp.sum(jax.nn.silu(pre), axis=2))
    return feats + mask[:, :, None, None] * jnp.einsum('pnbh,hg->pnbg', agg, w_u, precision=HIGH)

def forward(nodes, w_send, w_recv, w_update, w_edge, bias, w_out, edges, adjacency, boundary, assign, coarse_adj, coarse_edges, counts, targets):
    feats = nodes.reshape(N_DOM, NBD, B, H)
    adj = adjacency.reshape(N_DOM, NBD, K)
    edge = edges.reshape(N_DOM, NBD, K, B)
    sends = boundary.reshape(N_DOM, 2, NH)
    mask = (jnp.arange(NBD, dtype=jnp.int32)[None, :] < counts[:, None]).astype(jnp.float32)
    for level in range(2):
        feats = layer(feats, adj, edge, pick_rows(feats, sends[:, 0]), pick_rows(feats, sends[:, 1]), w_send[level], w_recv[level], w_update[level], w_edge[level], bias[level], mask)
    flat = feats.reshape(N_DOM, NBD * B, H)
    targets_of = assign.reshape(N_DOM, NBD * B)
    partial_sums = jax.vmap(lambda rows, seg: jax.ops.segment_sum(rows, seg, 3 * NCD))(flat, targets_of)
    coarse = (partial_sums[:, :NCD] + shift_dev(partial_sums[:, 2 * NCD:], 1) + shift_dev(partial_sums[:, NCD:2 * NCD], -1)) / 8.0
    cfeat = coarse.reshape(N_DOM, NCB, B, H)
    cmask = jnp.ones((N_DOM, NCB), jnp.float32)
    cfeat = layer(cfeat, coarse_adj.reshape(N_DOM, NCB, KC), coarse_edges.reshape(N_DOM, NCB, KC, B), cfeat, cfeat, w_send[2], w_recv[2], w_update[2], w_edge[2], bias[2], cmask)
    cflat = cfeat.reshape(N_DOM, NCD, H)
    cext = jnp.concatenate([cflat, shift_dev(cflat, 1), shift_dev(cflat, -1)], 1)
    fine = flat + pick_rows(cext, targets_of)
    pred = jnp.einsum('oh,pnh->pon', w_out, fine, precision=HIGH)
    target_dev = targets.reshape(4, N_DOM, NBD * B).transpose(1, 0, 2)
    live = jnp.repeat(mask, B, axis=1)
    error = pred - target_dev
    total = jnp.sum(counts).astype(jnp.float32) * B
    return jnp.sum(live[:, None, :] * error * error) / (4.0 * total)

def reference(nodes, edges, adjacency, boundary, assign, coarse_adj, coarse_edges, counts, targets, w_send, w_recv, w_update, w_edge, bias, w_out):
    value_grad = jax.value_and_grad(forward, argnums=(0, 1, 2, 3, 4, 5, 6))
    loss, grads = value_grad(nodes, w_send, w_recv, w_update, w_edge, bias, w_out, edges, adjacency, boundary, assign, coarse_adj, coarse_edges, counts, targets)
    return (loss.reshape(1), grads[0], grads[1], grads[2], grads[3], grads[4], grads[5], grads[6])
```

```python
import functools

import jax
import jax.numpy as jnp
from jax import lax
from jax.experimental import pallas as pl
from jax.experimental.pallas import tpu as pltpu
from jax.sharding import PartitionSpec as P

F32 = jnp.float32
BF16 = jnp.bfloat16
W = 128


def split(x):
    hi = x.astype(BF16)
    lo = (x - hi.astype(F32)).astype(BF16)
    return hi, lo


def stacked(x):
    return jnp.concatenate(split(x), axis=0)


def doubled(w):
    hi, lo = split(w)
    return jnp.concatenate([jnp.concatenate([hi, hi], 1), jnp.concatenate([lo, lo], 1)], 0)


def dot(a, b):
    return lax.dot_general(a, b, (((1,), (0,)), ((), ())), preferred_element_type=F32)


def dot_t(a, b):
    return lax.dot_general(a, b, (((1,), (1,)), ((), ())), preferred_element_type=F32)


def halves(r):
    m = r.shape[0] // 2
    return r[:m] + r[m:]


def quads(r):
    r = halves(r)
    return r[:, :W] + r[:, W:]


def group(ref, i, g):
    return jnp.concatenate([ref[g * i + j] for j in range(g)], axis=1) if g > 1 else ref[i]


def cols(x, j):
    return x[:, j * W:(j + 1) * W]


def kernel(N, nb, nc, K, KC, R, off,
           meta, nodes, edges, assign, cedges, targets, ws, wr, wu, we, bias, wo,
           dn, gs_o, gr_o, gu_o, ge_o, gb_o, go_o, loss_o,
           h0, h1, h2, c0, c1, own, recv, D0, D1, D2, agg0, agg1, agg2, G, S, gr, gc,
           oh, h2s, WF, WU, WUb, WSb, WRb, WE, BI, eacc, bacc, xb, st, xs, sts, t8, w8, gp, acc, rsb, res,
           ssem, rsem, sssem, srsem, assem, arsem):
    me = lax.axis_index("dom")
    steps = N.bit_length() - 1
    n = nb * W
    ncd = nc * W
    up_ok = me < N - 1
    down_ok = me > 0

    def partner(s):
        bit = 1 << s
        return me + bit * (1 - 2 * ((me // bit) % 2))

    def dev(d):
        return {"dom": d}

    MESH = pl.DeviceIdType.MESH

    @pl.when(me == 0)
    def _():
        for x in range(8):
            xb[x, 0:2] = jnp.zeros((2, W, W), F32)
        for x in range(2):
            xs[x, 0] = jnp.zeros(xs.shape[2:], F32)

    @pl.when(me == N - 1)
    def _():
        for x in range(8):
            xb[x, 2:4] = jnp.zeros((2, W, W), F32)
        for x in range(2):
            xs[x, 1] = jnp.zeros(xs.shape[2:], F32)

    barrier = pltpu.get_barrier_semaphore()
    for d in [lax.rem(me + 1, N), lax.rem(me + N - 1, N)] + [partner(s) for s in range(steps)]:
        pl.semaphore_signal(barrier, inc=1, device_id=dev(d), device_id_type=MESH)

    def copy_to(x, small, side):
        buf, stage, a, b = (xs, sts, sssem, srsem) if small else (xb, st, ssem, rsem)
        at = side if small else pl.ds(2 * side, 2)
        return pltpu.make_async_remote_copy(
            stage.at[x, at], buf.at[x, at], a.at[x, side], b.at[x, side],
            device_id=dev(me + 1 - 2 * side), device_id_type=MESH)

    def start(x, small=False):
        @pl.when(up_ok)
        def _():
            copy_to(x, small, 0).start()

        @pl.when(down_ok)
        def _():
            copy_to(x, small, 1).start()

    def wait(x, small=False):
        @pl.when(up_ok)
        def _():
            copy_to(x, small, 0).wait_send()
            copy_to(x, small, 1).wait_recv()

        @pl.when(down_ok)
        def _():
            copy_to(x, small, 1).wait_send()
            copy_to(x, small, 0).wait_recv()

    count = meta[off["count"]]

    def live(b):
        return jnp.where(b < count, 1.0, 0.0).astype(F32)

    def one(b):
        return None

    def by(m, v):
        return v if m is None else v * m

    def tr(b, _):
        h0[b] = nodes[b].T
        return 0

    lax.fori_loop(0, nb, tr, 0)

    def stage_boundary(x, h):
        for j in range(2):
            st[x, j] = h[meta[off["boundary"] + j]]
            st[x, 2 + j] = h[meta[off["boundary"] + 2 + j]]

    stage_boundary(0, h0)
    pl.semaphore_wait(barrier, 2 + steps)
    start(0)

    def prep(l, _):
        WF[l, 0:256] = doubled(ws[l].T * 0.5)
        WF[l, 256:512] = doubled(wr[l].T * 0.5)
        WU[l] = doubled(wu[l].T)
        WUb[l] = doubled(wu[l])
        WSb[l] = doubled(ws[l])
        WRb[l] = doubled(wr[l])
        return 0

    lax.fori_loop(0, 3, prep, 0)
    for l in range(3):
        WE[l] = jnp.broadcast_to(we[l:l + 1, :] * 0.5, (W, W)).T
        BI[l] = jnp.broadcast_to(bias[l:l + 1, :] * 0.5, (W, W)).T
    acc[...] = jnp.zeros_like(acc)

    def project(l, nblk, h):
        g = min(4, nblk)

        def body(i, _):
            r = dot(WF[l], stacked(group(h, i, g)))
            o, v = halves(r[:256]), halves(r[256:])
            for j in range(g):
                own[g * i + j] = cols(o, j) + BI[l]
                recv[g * i + j] = cols(v, j)
            return 0

        lax.fori_loop(0, nblk // g, body, 0)

    def messages(l, nblk, k_, h, hn, D, agg, x, adj, ed, mask):
        v = halves(dot(WF[l, 256:512], stacked(group(xb.at[x], 0, 4))))
        for j in range(4):
            recv[nblk + j] = cols(v, j)

        def body(i, _):
            sums = []
            for j in range(2):
                b = 2 * i + j
                o = own[b]
                a = None
                for k in range(k_):
                    q = o + recv[meta[adj + b * k_ + k]] + WE[l] * ed[b, pl.ds(k, 1), :]
                    t = jnp.tanh(q)
                    qt = q * t
                    D[b * k_ + k] = (0.5 + 0.5 * t) * ((1.0 + q) - qt)
                    a = q + qt if a is None else a + (q + qt)
                agg[b] = a
                sums.append(a)
            u = halves(dot(WU[l], stacked(jnp.concatenate(sums, 1))))
            for j in range(2):
                b = 2 * i + j
                hn[b] = h[b] + by(mask(b), cols(u, j))
            return 0

        lax.fori_loop(0, nblk // 2, body, 0)

    def add_acc(row, value):
        acc[row:row + W] += value

    def backward(l, nblk, k_, h, go, D, agg, x, y, pre, ed, mask):
        base = 3 * W * l
        eacc[...] = jnp.zeros_like(eacc)
        bacc[...] = jnp.zeros_like(bacc)

        def body(i, _):
            bs = [2 * i, 2 * i + 1]
            us = stacked(jnp.concatenate([by(mask(b), go[b]) for b in bs], 1))
            ga = halves(dot(WUb[l], us))
            add_acc(base + 2 * W, quads(dot_t(stacked(group(agg, i, 2)), us)))
            sums = []
            for j, b in enumerate(bs):
                gj = cols(ga, j)
                s = e = None
                for k in range(k_):
                    m = gj * D[b * k_ + k]
                    G[b * k_ + k] = m
                    w = m * ed[b, pl.ds(k, 1), :]
                    s = m if s is None else s + m
                    e = w if e is None else e + w
                eacc[...] += e
                bacc[...] += s
                sums.append(s)
            ss = stacked(jnp.concatenate(sums, 1))
            add_acc(base, quads(dot_t(stacked(group(h, i, 2)), ss)))
            f = halves(dot(WSb[l], ss))
            for j, b in enumerate(bs):
                go[b] = go[b] + cols(f, j)
            return 0

        lax.fori_loop(0, nblk // 2, body, 0)
        small = 9 * W
        acc[small + l:small + l + 1] = jnp.sum(eacc[...].T, axis=0, keepdims=True)
        acc[small + 3 + l:small + 4 + l] = jnp.sum(bacc[...].T, axis=0, keepdims=True)

        def scan(j, run):
            run = run * meta[off[pre + "same"] + j].astype(F32) + G[meta[off[pre + "order"] + j]]
            S[j] = run
            return run

        lax.fori_loop(0, nblk * k_, scan, jnp.zeros((W, W), F32))

        def ext(e):
            return S[meta[off[pre + "end"] + e]] * meta[off[pre + "flag"] + e].astype(F32)

        xsx = stacked(jnp.concatenate([ext(nblk + j) for j in range(4)], 1))
        v = halves(dot(WRb[l], xsx))
        for j in range(2):
            st[y, 2 + j] = cols(v, j)
            st[y, j] = cols(v, 2 + j)
        start(y)
        add_acc(base + W, quads(dot_t(stacked(group(xb.at[x], 0, 4)), xsx)))
        g = min(4, nblk)

        def rest(i, _):
            es = stacked(jnp.concatenate([ext(g * i + j) for j in range(g)], 1))
            f = halves(dot(WRb[l], es))
            for j in range(g):
                go[g * i + j] = go[g * i + j] + cols(f, j)
            add_acc(base + W, quads(dot_t(stacked(group(h, i, g)), es)))
            return 0

        lax.fori_loop(0, nblk // g, rest, 0)
        wait(y)

    def returned(go, y, b):
        v = go[b]
        for j in range(2):
            v = v + xb[y, j] * jnp.where(meta[off["boundary"] + 2 + j] == b, 1.0, 0.0).astype(F32)
            v = v + xb[y, 2 + j] * jnp.where(meta[off["boundary"] + j] == b, 1.0, 0.0).astype(F32)
        return v

    project(0, nb, h0)

    def onehot(i, _):
        rows = lax.broadcasted_iota(jnp.int32, (W, n), 0) + i * W
        oh[pl.ds(pl.multiple_of(i * W, W), W), :] = jnp.where(rows == assign[...], 1.0, 0.0).astype(BF16)
        return 0

    lax.fori_loop(0, 3 * nc, onehot, 0)
    wait(0)
    messages(0, nb, K, h0, h1, D0, agg0, 0, off["adj"], edges, live)
    stage_boundary(1, h1)
    start(1)
    project(1, nb, h1)
    wait(1)
    messages(1, nb, K, h1, h2, D1, agg1, 1, off["adj"], edges, live)

    for b in range(nb):
        h2s[:, b * W:(b + 1) * W] = stacked(h2[b])

    def restricted(c):
        return halves(dot_t(h2s[...], oh[c * ncd:(c + 1) * ncd, :]))

    v = restricted(1)
    for j in range(nc):
        st[2, 2 + j] = cols(v, j)
    v = restricted(2)
    for j in range(nc):
        st[2, j] = cols(v, j)
    start(2)
    v = restricted(0)
    w8[...] = jnp.zeros_like(w8)
    w8[0:4] = wo[...]
    t8[...] = jnp.zeros_like(t8)
    t8[0:4] = targets[...]
    whi, wlo = split(w8[...])
    whi, wlo = whi.astype(F32), wlo.astype(F32)
    wd = jnp.concatenate([jnp.concatenate([whi, whi], 1), jnp.concatenate([wlo, wlo], 1)], 0).astype(BF16)
    fill = jnp.zeros((W - 16, W), F32)
    wt = jnp.concatenate([jnp.concatenate([whi, whi, fill], 0).T, jnp.concatenate([wlo, wlo, fill], 0).T], 0).astype(BF16)

    def rows16(x):
        hi, lo = split(x)
        return jnp.concatenate([hi.astype(F32), lo.astype(F32)], 0)

    wait(2)
    for j in range(nc):
        c0[j] = (cols(v, j) + xb[2, j] + xb[2, 2 + j]) * 0.125
        st[3, j] = c0[j]
        st[3, 2 + j] = c0[j]
    start(3)
    project(2, nc, c0)
    wait(3)
    messages(2, nc, KC, c0, c1, D2, agg2, 3, off["cadj"], cedges, one)

    c1s = stacked(group(c1, 0, nc))
    pc = halves(dot(wd, c1s))
    sts[0, 0] = pc
    sts[0, 1] = pc
    start(0, True)
    pred = halves(dot(wd, h2s[...])) + halves(dot(rows16(pc).astype(BF16), oh[0:ncd, :]))
    wait(0, True)
    pn = jnp.concatenate([rows16(xs[0, 0]), rows16(xs[0, 1])], 1).astype(BF16)
    pred = pred + halves(dot(pn, oh[ncd:3 * ncd, :]))
    err = jnp.where(lax.broadcasted_iota(jnp.int32, (8, n), 1) < count * W, pred - t8[...], 0.0)
    small = 9 * W
    e2 = err * err
    tot = e2[:, :W]
    for b in range(1, nb):
        tot = tot + cols(e2, b)
    acc[small + 10:small + 11] = jnp.broadcast_to(jnp.sum(tot).reshape(1, 1), (1, W))
    acc[small + 11:small + 12] = jnp.broadcast_to(count.astype(F32), (1, W))
    gp[...] = err * (2.0 / (4.0 * W * nb * N))
    g16 = rows16(gp[...])
    g16b = g16.astype(BF16)
    gq = halves(dot_t(g16b, oh[ncd:3 * ncd, :]))
    sts[1, 1] = gq[:, :ncd]
    sts[1, 0] = gq[:, ncd:]
    start(1, True)
    gq = halves(dot_t(g16b, oh[0:ncd, :]))
    go8 = quads(dot_t(g16b, h2s[...]))
    wait(1, True)
    gq = gq + xs[1, 0] + xs[1, 1]
    q16 = rows16(gq)
    go8 = go8 + quads(dot_t(q16.astype(BF16), c1s))
    acc[small + 6:small + 10] = go8[0:4]
    f = halves(dot(wt, jnp.concatenate([q16, jnp.zeros((W - 16, ncd), F32)], 0).astype(BF16)))
    for j in range(nc):
        gc[j] = cols(f, j)

    backward(2, nc, KC, c0, gc, D2, agg2, 3, 4, "c", cedges, one)
    for j in range(nc):
        v = (gc[j] + xb[4, j] + xb[4, 2 + j]) * 0.125
        st[5, j] = v
        st[5, 2 + j] = v
    start(5)
    gp128 = jnp.concatenate([g16, jnp.zeros((W - 16, n), F32)], 0).astype(BF16)
    f = halves(dot(wt, gp128))
    f = f + halves(dot(stacked(jnp.concatenate([st[5, j] for j in range(nc)], 1)), oh[0:ncd, :]))
    wait(5)
    f = f + halves(dot(stacked(group(xb.at[5], 0, 4)), oh[ncd:3 * ncd, :]))
    for b in range(nb):
        gr[b] = cols(f, b)

    backward(1, nb, K, h1, gr, D1, agg1, 1, 6, "", edges, live)

    def ret(b, _):
        gr[b] = returned(gr, 6, b)
        return 0

    lax.fori_loop(0, nb, ret, 0)
    backward(0, nb, K, h0, gr, D0, agg0, 0, 7, "", edges, live)

    lo = 0 * me
    size = R
    spot = 0
    for s in range(steps):
        size //= 2
        mine = (me // (1 << s)) % 2
        copy = pltpu.make_async_remote_copy(
            acc.at[pl.ds(pl.multiple_of(lo + (1 - mine) * size, 8), size)], rsb.at[pl.ds(spot, size)],
            assem.at[s], arsem.at[s], device_id=dev(partner(s)), device_id_type=MESH)
        copy.start()
        if s == 0:
            def fin(b, _):
                gr[b] = returned(gr, 7, b).T
                return 0

            lax.fori_loop(0, nb, fin, 0)
        copy.wait()
        lo = lo + mine * size
        keep = pl.ds(pl.multiple_of(lo, 8), size)
        acc[keep] += rsb[pl.ds(spot, size)]
        spot += size
    keep = pl.ds(pl.multiple_of(lo, 8), size)
    res[keep] = acc[keep]
    for s in range(steps - 1, -1, -1):
        mine = (me // (1 << s)) % 2
        part = res.at[pl.ds(pl.multiple_of(lo, 8), size)]
        copy = pltpu.make_async_remote_copy(
            part, part, assem.at[steps + s], arsem.at[steps + s], device_id=dev(partner(s)), device_id_type=MESH)
        copy.start()
        copy.wait()
        lo = lo - mine * size
        size *= 2

    total = res[small + 11:small + 12]
    ratio = (1.0 * nb * N) / total
    for l in range(3):
        gs_o[l] = res[3 * W * l:3 * W * l + W] * ratio
        gr_o[l] = res[3 * W * l + W:3 * W * l + 2 * W] * ratio
        gu_o[l] = res[3 * W * l + 2 * W:3 * W * l + 3 * W] * ratio
    ge_o[...] = res[small:small + 3] * ratio
    gb_o[...] = res[small + 3:small + 6] * ratio
    go_o[...] = res[small + 6:small + 10] * ratio
    loss_o[...] = res[small + 10:small + 11] / (4.0 * W * total)

    def out(b, _):
        dn[b] = gr[b] * ratio
        return 0

    lax.fori_loop(0, nb, out, 0)


def sort_info(adj, ext):
    a = adj.reshape(-1)
    m = a.shape[0]
    i = jnp.arange(m, dtype=jnp.int32)
    rank = jnp.sum(((a[None, :] < a[:, None]) | ((a[None, :] == a[:, None]) & (i[None, :] < i[:, None]))).astype(jnp.int32), 1)
    hit = rank[None, :] == i[:, None]
    order = jnp.sum(jnp.where(hit, i[None, :], 0), 1)
    value = jnp.sum(jnp.where(hit, a[None, :], 0), 1)
    before = jnp.sum(jnp.where(rank[None, :] == i[:, None] - 1, a[None, :], 0), 1)
    same = ((value == before) & (i > 0)).astype(jnp.int32)
    e = jnp.arange(ext, dtype=jnp.int32)
    end = jnp.maximum(jnp.sum((a[None, :] <= e[:, None]).astype(jnp.int32), 1) - 1, 0)
    flag = (jnp.sum((a[None, :] == e[:, None]).astype(jnp.int32), 1) > 0).astype(jnp.int32)
    return order, same, end, flag


def local(N, nodes, edges, adjacency, boundary, assign, coarse_adj, coarse_edges, counts, targets, ws, wr, wu, we, bias, wo):
    nb, K, _ = edges.shape
    nc, KC, _ = coarse_edges.shape
    n = nb * W
    ncd = nc * W
    steps = N.bit_length() - 1
    unit = 8 * N
    R = -(-(9 * W + 12) // unit) * unit
    order, same, end, flag = sort_info(adjacency, nb + 4)
    corder, csame, cend, cflag = sort_info(coarse_adj, 3 * nc)
    parts = {"adj": adjacency.reshape(-1), "boundary": boundary.reshape(-1), "count": counts, "cadj": coarse_adj.reshape(-1),
             "order": order, "same": same, "end": end, "flag": flag, "corder": corder, "csame": csame, "cend": cend, "cflag": cflag}
    off, at = {}, 0
    for name, value in parts.items():
        off[name] = at
        at += value.shape[0]
    meta = jnp.concatenate(list(parts.values()))
    vm = pl.BlockSpec(memory_space=pltpu.VMEM)
    blk = lambda m: pltpu.VMEM((m, W, W), F32)
    b16 = lambda *s: pltpu.VMEM(s, BF16)
    f32 = lambda *s: pltpu.VMEM(s, F32)
    sd = lambda *s: jax.ShapeDtypeStruct(s, F32)
    outs = pl.pallas_call(
        functools.partial(kernel, N, nb, nc, K, KC, R, off),
        out_shape=(sd(nb, W, W), sd(3, W, W), sd(3, W, W), sd(3, W, W), sd(3, W), sd(3, W), sd(4, W), sd(1, W)),
        in_specs=[pl.BlockSpec(memory_space=pltpu.SMEM)] + [vm] * 11,
        out_specs=(vm,) * 8,
        scratch_shapes=[
            blk(nb), blk(nb), blk(nb), blk(nc), blk(nc), blk(nb), blk(nb + 4),
            blk(nb * K), blk(nb * K), blk(nc * KC), blk(nb), blk(nb), blk(nc), blk(nb * K), blk(nb * K), blk(nb), blk(nc),
            b16(3 * ncd, n), b16(2 * W, n), b16(3, 512, 256), b16(3, 256, 256), b16(3, 256, 256), b16(3, 256, 256), b16(3, 256, 256),
            blk(3), blk(3), f32(W, W), f32(W, W), f32(8, 4, W, W), f32(8, 4, W, W), f32(2, 2, 8, ncd), f32(2, 2, 8, ncd),
            f32(8, n), f32(8, W), f32(8, n), f32(R, W), f32(R, W), f32(R, W),
            pltpu.SemaphoreType.DMA((8, 2)), pltpu.SemaphoreType.DMA((8, 2)), pltpu.SemaphoreType.DMA((2, 2)), pltpu.SemaphoreType.DMA((2, 2)),
            pltpu.SemaphoreType.DMA((2 * steps,)), pltpu.SemaphoreType.DMA((2 * steps,)),
        ],
        compiler_params=pltpu.CompilerParams(collective_id=0, has_side_effects=True, vmem_limit_bytes=56 * 1024 * 1024),
    )(meta, nodes.reshape(nb, W, W), edges, assign.reshape(1, n), coarse_edges, targets, ws, wr, wu, we, bias, wo)
    return (outs[7][0, :1], outs[0].reshape(n, W)) + outs[1:7]


def solution(mesh):
    both = ("groups", "dom")
    in_specs = (
        P(both, None), P(both, None, None), P(both, None), P(both, None), P(both), P(both, None), P(both, None, None), P(both),
        P(None, both), P(), P(), P(), P(), P(), P(),
    )
    out_specs = (
        P("groups"), P(both, None), P("groups", None, None), P("groups", None, None), P("groups", None, None),
        P("groups", None), P("groups", None), P("groups", None),
    )
    return jax.shard_map(functools.partial(local, mesh.shape["dom"]), mesh=mesh, in_specs=in_specs, out_specs=out_specs, check_vma=False)
```

```python
import functools

import jax
import jax.numpy as jnp
from jax import lax
from jax.experimental import pallas as pl
from jax.experimental.pallas import tpu as pltpu
from jax.sharding import PartitionSpec as P

F32 = jnp.float32
BF16 = jnp.bfloat16
W = 128


def split(x):
    hi = x.astype(BF16)
    lo = (x - hi.astype(F32)).astype(BF16)
    return hi, lo


def stacked(x):
    return jnp.concatenate(split(x), axis=0)


def doubled(w):
    hi, lo = split(w)
    return jnp.concatenate([jnp.concatenate([hi, hi], 1), jnp.concatenate([lo, lo], 1)], 0)


def dot(a, b):
    return lax.dot_general(a, b, (((1,), (0,)), ((), ())), preferred_element_type=F32)


def dot_t(a, b):
    return lax.dot_general(a, b, (((1,), (1,)), ((), ())), preferred_element_type=F32)


def halves(r):
    m = r.shape[0] // 2
    return r[:m] + r[m:]


def quads(r):
    r = halves(r)
    return r[:, :W] + r[:, W:]


def group(ref, i, g):
    return jnp.concatenate([ref[g * i + j] for j in range(g)], axis=1) if g > 1 else ref[i]


def cols(x, j):
    return x[:, j * W:(j + 1) * W]


def kernel(N, nb, nc, K, KC, RA, RB, off,
           meta, nodes, edges, assign, cedges, targets, ws, wr, wu, we, bias, wo,
           dn, res_o,
           h0, h1, h2, c0, c1, own, recv, D0, D1, D2, agg0, agg1, agg2, G, S, gr, gc,
           oh, h2s, WF, WU, WUb, WSb, WRb, WE, BI, eacc, bacc, xb, st, xs, sts, t8, w8, gp, acc, rsb, res,
           ssem, rsem, sssem, srsem, assem, arsem):
    me = lax.axis_index("dom")
    steps = N.bit_length() - 1
    n = nb * W
    ncd = nc * W
    up_ok = me < N - 1
    down_ok = me > 0

    def partner(s):
        bit = 1 << s
        return me + bit * (1 - 2 * ((me // bit) % 2))

    def dev(d):
        return {"dom": d}

    MESH = pl.DeviceIdType.MESH

    @pl.when(me == 0)
    def _():
        for x in range(8):
            xb[x, 0:2] = jnp.zeros((2, W, W), F32)
        for x in range(2):
            xs[x, 0] = jnp.zeros(xs.shape[2:], F32)

    @pl.when(me == N - 1)
    def _():
        for x in range(8):
            xb[x, 2:4] = jnp.zeros((2, W, W), F32)
        for x in range(2):
            xs[x, 1] = jnp.zeros(xs.shape[2:], F32)

    barrier = pltpu.get_barrier_semaphore()
    for d in [lax.rem(me + 1, N), lax.rem(me + N - 1, N)] + [partner(s) for s in range(steps)]:
        pl.semaphore_signal(barrier, inc=1, device_id=dev(d), device_id_type=MESH)

    def copy_to(x, small, side):
        buf, stage, a, b = (xs, sts, sssem, srsem) if small else (xb, st, ssem, rsem)
        at = side if small else pl.ds(2 * side, 2)
        return pltpu.make_async_remote_copy(
            stage.at[x, at], buf.at[x, at], a.at[x, side], b.at[x, side],
            device_id=dev(me + 1 - 2 * side), device_id_type=MESH)

    def start(x, small=False):
        @pl.when(up_ok)
        def _():
            copy_to(x, small, 0).start()

        @pl.when(down_ok)
        def _():
            copy_to(x, small, 1).start()

    def wait(x, small=False):
        @pl.when(up_ok)
        def _():
            copy_to(x, small, 0).wait_send()
            copy_to(x, small, 1).wait_recv()

        @pl.when(down_ok)
        def _():
            copy_to(x, small, 1).wait_send()
            copy_to(x, small, 0).wait_recv()

    count = meta[off["count"]]

    def live(b):
        return jnp.where(b < count, 1.0, 0.0).astype(F32)

    def one(b):
        return None

    def by(m, v):
        return v if m is None else v * m

    def tr(b, _):
        h0[b] = nodes[b].T
        return 0

    lax.fori_loop(0, nb, tr, 0)

    def stage_boundary(x, h):
        for j in range(2):
            st[x, j] = h[meta[off["boundary"] + j]]
            st[x, 2 + j] = h[meta[off["boundary"] + 2 + j]]

    stage_boundary(0, h0)
    pl.semaphore_wait(barrier, 2 + steps)
    start(0)

    def prep(l, _):
        WF[l, 0:256] = doubled(ws[l].T * 0.5)
        WF[l, 256:512] = doubled(wr[l].T * 0.5)
        WU[l] = doubled(wu[l].T)
        WUb[l] = doubled(wu[l])
        WSb[l] = doubled(ws[l])
        WRb[l] = doubled(wr[l])
        return 0

    lax.fori_loop(0, 3, prep, 0)
    for l in range(3):
        WE[l] = jnp.broadcast_to(we[l:l + 1, :] * 0.5, (W, W)).T
        BI[l] = jnp.broadcast_to(bias[l:l + 1, :] * 0.5, (W, W)).T
    acc[...] = jnp.zeros_like(acc)

    def project(l, nblk, h):
        g = min(4, nblk)

        def body(i, _):
            r = dot(WF[l], stacked(group(h, i, g)))
            o, v = halves(r[:256]), halves(r[256:])
            for j in range(g):
                own[g * i + j] = cols(o, j) + BI[l]
                recv[g * i + j] = cols(v, j)
            return 0

        lax.fori_loop(0, nblk // g, body, 0, unroll=True)

    def messages(l, nblk, k_, h, hn, D, agg, x, adj, ed, mask):
        v = halves(dot(WF[l, 256:512], stacked(group(xb.at[x], 0, 4))))
        for j in range(4):
            recv[nblk + j] = cols(v, j)

        def body(i, _):
            sums = []
            for j in range(2):
                b = 2 * i + j
                o = own[b]
                a = None
                for k in range(k_):
                    q = o + recv[meta[adj + b * k_ + k]] + WE[l] * ed[b, pl.ds(k, 1), :]
                    t = jnp.tanh(q)
                    qt = q * t
                    D[b * k_ + k] = (0.5 + 0.5 * t) * ((1.0 + q) - qt)
                    a = q + qt if a is None else a + (q + qt)
                agg[b] = a
                sums.append(a)
            u = halves(dot(WU[l], stacked(jnp.concatenate(sums, 1))))
            for j in range(2):
                b = 2 * i + j
                hn[b] = h[b] + by(mask(b), cols(u, j))
            return 0

        lax.fori_loop(0, nblk // 2, body, 0, unroll=2)

    base_of = {0: RA, 1: 0, 2: 3 * W}
    ge_of = {0: RA + 3 * W, 1: 6 * W, 2: 6 * W + 1}
    gb_of = {0: RA + 3 * W + 1, 1: 6 * W + 2, 2: 6 * W + 3}

    def add_acc(row, value):
        acc[row:row + W] += value

    def backward(l, nblk, k_, h, go, D, agg, x, y, pre, ed, mask, hook=None):
        base = base_of[l]
        hook = hook or (lambda: None)
        eacc[...] = jnp.zeros_like(eacc)
        bacc[...] = jnp.zeros_like(bacc)

        def body(i, _):
            bs = [2 * i, 2 * i + 1]
            us = stacked(jnp.concatenate([by(mask(b), go[b]) for b in bs], 1))
            ga = halves(dot(WUb[l], us))
            add_acc(base + 2 * W, quads(dot_t(stacked(group(agg, i, 2)), us)))
            sums = []
            for j, b in enumerate(bs):
                gj = cols(ga, j)
                s = e = None
                for k in range(k_):
                    m = gj * D[b * k_ + k]
                    G[b * k_ + k] = m
                    w = m * ed[b, pl.ds(k, 1), :]
                    s = m if s is None else s + m
                    e = w if e is None else e + w
                eacc[...] += e
                bacc[...] += s
                sums.append(s)
            ss = stacked(jnp.concatenate(sums, 1))
            add_acc(base, quads(dot_t(stacked(group(h, i, 2)), ss)))
            f = halves(dot(WSb[l], ss))
            for j, b in enumerate(bs):
                go[b] = go[b] + cols(f, j)
            return 0

        hook()
        pairs = nblk // 2
        lax.fori_loop(0, pairs // 2, body, 0, unroll=2)
        hook()
        lax.fori_loop(pairs // 2, pairs, body, 0, unroll=2)
        hook()
        acc[ge_of[l]:ge_of[l] + 1] = jnp.sum(eacc[...].T, axis=0, keepdims=True)
        acc[gb_of[l]:gb_of[l] + 1] = jnp.sum(bacc[...].T, axis=0, keepdims=True)

        def scan(j, run):
            run = run * meta[off[pre + "same"] + j].astype(F32) + G[meta[off[pre + "order"] + j]]
            S[j] = run
            return run

        half = nblk * k_ // 2
        run = lax.fori_loop(0, half, scan, jnp.zeros((W, W), F32), unroll=8)
        hook()
        lax.fori_loop(half, nblk * k_, scan, run, unroll=8)
        hook()

        def ext(e):
            return S[meta[off[pre + "end"] + e]] * meta[off[pre + "flag"] + e].astype(F32)

        xsx = stacked(jnp.concatenate([ext(nblk + j) for j in range(4)], 1))
        v = halves(dot(WRb[l], xsx))
        for j in range(2):
            st[y, 2 + j] = cols(v, j)
            st[y, j] = cols(v, 2 + j)
        start(y)
        hook()
        add_acc(base + W, quads(dot_t(stacked(group(xb.at[x], 0, 4)), xsx)))
        g = min(4, nblk)

        def rest(i, _):
            es = stacked(jnp.concatenate([ext(g * i + j) for j in range(g)], 1))
            f = halves(dot(WRb[l], es))
            for j in range(g):
                go[g * i + j] = go[g * i + j] + cols(f, j)
            add_acc(base + W, quads(dot_t(stacked(group(h, i, g)), es)))
            return 0

        lax.fori_loop(0, nblk // g, rest, 0, unroll=True)
        hook()
        wait(y)

    def returned(go, y, b):
        v = go[b]
        for j in range(2):
            v = v + xb[y, j] * jnp.where(meta[off["boundary"] + 2 + j] == b, 1.0, 0.0).astype(F32)
            v = v + xb[y, 2 + j] * jnp.where(meta[off["boundary"] + j] == b, 1.0, 0.0).astype(F32)
        return v

    project(0, nb, h0)

    def onehot(i, _):
        rows = lax.broadcasted_iota(jnp.int32, (W, n), 0) + i * W
        oh[pl.ds(pl.multiple_of(i * W, W), W), :] = jnp.where(rows == assign[...], 1.0, 0.0).astype(BF16)
        return 0

    lax.fori_loop(0, 3 * nc, onehot, 0)
    wait(0)
    messages(0, nb, K, h0, h1, D0, agg0, 0, off["adj"], edges, live)
    stage_boundary(1, h1)
    start(1)
    project(1, nb, h1)
    wait(1)
    messages(1, nb, K, h1, h2, D1, agg1, 1, off["adj"], edges, live)

    for b in range(nb):
        h2s[:, b * W:(b + 1) * W] = stacked(h2[b])

    def restricted(c):
        return halves(dot_t(h2s[...], oh[c * ncd:(c + 1) * ncd, :]))

    v = restricted(1)
    for j in range(nc):
        st[2, 2 + j] = cols(v, j)
    v = restricted(2)
    for j in range(nc):
        st[2, j] = cols(v, j)
    start(2)
    v = restricted(0)
    w8[...] = jnp.zeros_like(w8)
    w8[0:4] = wo[...]
    t8[...] = jnp.zeros_like(t8)
    t8[0:4] = targets[...]
    whi, wlo = split(w8[...])
    whi, wlo = whi.astype(F32), wlo.astype(F32)
    wd = jnp.concatenate([jnp.concatenate([whi, whi], 1), jnp.concatenate([wlo, wlo], 1)], 0).astype(BF16)
    fill = jnp.zeros((W - 16, W), F32)
    wt = jnp.concatenate([jnp.concatenate([whi, whi, fill], 0).T, jnp.concatenate([wlo, wlo, fill], 0).T], 0).astype(BF16)

    def rows16(x):
        hi, lo = split(x)
        return jnp.concatenate([hi.astype(F32), lo.astype(F32)], 0)

    wait(2)
    for j in range(nc):
        c0[j] = (cols(v, j) + xb[2, j] + xb[2, 2 + j]) * 0.125
        st[3, j] = c0[j]
        st[3, 2 + j] = c0[j]
    start(3)
    project(2, nc, c0)
    wait(3)
    messages(2, nc, KC, c0, c1, D2, agg2, 3, off["cadj"], cedges, one)

    c1s = stacked(group(c1, 0, nc))
    pc = halves(dot(wd, c1s))
    sts[0, 0] = pc
    sts[0, 1] = pc
    start(0, True)
    pred = halves(dot(wd, h2s[...])) + halves(dot(rows16(pc).astype(BF16), oh[0:ncd, :]))
    wait(0, True)
    pn = jnp.concatenate([rows16(xs[0, 0]), rows16(xs[0, 1])], 1).astype(BF16)
    pred = pred + halves(dot(pn, oh[ncd:3 * ncd, :]))
    err = jnp.where(lax.broadcasted_iota(jnp.int32, (8, n), 1) < count * W, pred - t8[...], 0.0)
    small = 6 * W
    e2 = err * err
    tot = e2[:, :W]
    for b in range(1, nb):
        tot = tot + cols(e2, b)
    acc[small + 8:small + 9] = jnp.broadcast_to(jnp.sum(tot).reshape(1, 1), (1, W))
    acc[small + 9:small + 10] = jnp.broadcast_to(count.astype(F32), (1, W))
    gp[...] = err * (2.0 / (4.0 * W * nb * N))
    g16 = rows16(gp[...])
    g16b = g16.astype(BF16)
    gq = halves(dot_t(g16b, oh[ncd:3 * ncd, :]))
    sts[1, 1] = gq[:, :ncd]
    sts[1, 0] = gq[:, ncd:]
    start(1, True)
    gq = halves(dot_t(g16b, oh[0:ncd, :]))
    go8 = quads(dot_t(g16b, h2s[...]))
    wait(1, True)
    gq = gq + xs[1, 0] + xs[1, 1]
    q16 = rows16(gq)
    go8 = go8 + quads(dot_t(q16.astype(BF16), c1s))
    acc[small + 4:small + 8] = go8[0:4]
    f = halves(dot(wt, jnp.concatenate([q16, jnp.zeros((W - 16, ncd), F32)], 0).astype(BF16)))
    for j in range(nc):
        gc[j] = cols(f, j)

    backward(2, nc, KC, c0, gc, D2, agg2, 3, 4, "c", cedges, one)
    for j in range(nc):
        v = (gc[j] + xb[4, j] + xb[4, 2 + j]) * 0.125
        st[5, j] = v
        st[5, 2 + j] = v
    start(5)
    gp128 = jnp.concatenate([g16, jnp.zeros((W - 16, n), F32)], 0).astype(BF16)
    f = halves(dot(wt, gp128))
    f = f + halves(dot(stacked(jnp.concatenate([st[5, j] for j in range(nc)], 1)), oh[0:ncd, :]))
    wait(5)
    f = f + halves(dot(stacked(group(xb.at[5], 0, 4)), oh[ncd:3 * ncd, :]))
    for b in range(nb):
        gr[b] = cols(f, b)

    backward(1, nb, K, h1, gr, D1, agg1, 1, 6, "", edges, live)

    def ret(b, _):
        gr[b] = returned(gr, 6, b)
        return 0

    lax.fori_loop(0, nb, ret, 0)

    def summed(base, rows, q):
        lo, size, spot = base + 0 * me, rows, base
        for s in range(steps):
            size //= 2
            mine = (me // (1 << s)) % 2
            copy = pltpu.make_async_remote_copy(
                acc.at[pl.ds(pl.multiple_of(lo + (1 - mine) * size, 8), size)], rsb.at[pl.ds(spot, size)],
                assem.at[q + s], arsem.at[q + s], device_id=dev(partner(s)), device_id_type=MESH)
            copy.start()
            yield
            copy.wait()
            lo = lo + mine * size
            keep = pl.ds(pl.multiple_of(lo, 8), size)
            acc[keep] += rsb[pl.ds(spot, size)]
            spot += size
        res[keep] = acc[keep]
        for s in range(steps - 1, -1, -1):
            mine = (me // (1 << s)) % 2
            part = res.at[pl.ds(pl.multiple_of(lo, 8), size)]
            copy = pltpu.make_async_remote_copy(
                part, part, assem.at[q + steps + s], arsem.at[q + steps + s], device_id=dev(partner(s)), device_id_type=MESH)
            copy.start()
            yield
            copy.wait()
            lo = lo - mine * size
            size *= 2

    early = summed(0, RA, 0)
    backward(0, nb, K, h0, gr, D0, agg0, 0, 7, "", edges, live, lambda: next(early, None))
    late = summed(RA, RB, 2 * steps)
    next(late)

    def fin(b, _):
        dn[b] = returned(gr, 7, b).T
        return 0

    lax.fori_loop(0, nb, fin, 0)
    for _ in range(2 * steps):
        next(early, None)
        next(late, None)
    res_o[...] = res[...]


def finish(nb, N, RA, gr, res, dn, gs_o, gr_o, gu_o, ge_o, gb_o, go_o, loss_o):
    small = 6 * W
    total = res[small + 9:small + 10]
    ratio = (1.0 * nb * N) / total
    for l, base in ((0, RA), (1, 0), (2, 3 * W)):
        gs_o[l] = res[base:base + W] * ratio
        gr_o[l] = res[base + W:base + 2 * W] * ratio
        gu_o[l] = res[base + 2 * W:base + 3 * W] * ratio
    ge_o[0:1] = res[RA + 3 * W:RA + 3 * W + 1] * ratio
    ge_o[1:3] = res[small:small + 2] * ratio
    gb_o[0:1] = res[RA + 3 * W + 1:RA + 3 * W + 2] * ratio
    gb_o[1:3] = res[small + 2:small + 4] * ratio
    go_o[...] = res[small + 4:small + 8] * ratio
    loss_o[...] = res[small + 8:small + 9] / (4.0 * W * total)

    def out(b, _):
        dn[b] = gr[b] * ratio
        return 0

    lax.fori_loop(0, nb, out, 0)


def sort_info(adj, ext):
    a = adj.reshape(-1)
    m = a.shape[0]
    i = jnp.arange(m, dtype=jnp.int32)
    rank = jnp.sum(((a[None, :] < a[:, None]) | ((a[None, :] == a[:, None]) & (i[None, :] < i[:, None]))).astype(jnp.int32), 1)
    hit = rank[None, :] == i[:, None]
    order = jnp.sum(jnp.where(hit, i[None, :], 0), 1)
    value = jnp.sum(jnp.where(hit, a[None, :], 0), 1)
    before = jnp.sum(jnp.where(rank[None, :] == i[:, None] - 1, a[None, :], 0), 1)
    same = ((value == before) & (i > 0)).astype(jnp.int32)
    e = jnp.arange(ext, dtype=jnp.int32)
    end = jnp.maximum(jnp.sum((a[None, :] <= e[:, None]).astype(jnp.int32), 1) - 1, 0)
    flag = (jnp.sum((a[None, :] == e[:, None]).astype(jnp.int32), 1) > 0).astype(jnp.int32)
    return order, same, end, flag


def local(N, nodes, edges, adjacency, boundary, assign, coarse_adj, coarse_edges, counts, targets, ws, wr, wu, we, bias, wo):
    nb, K, _ = edges.shape
    nc, KC, _ = coarse_edges.shape
    n = nb * W
    ncd = nc * W
    steps = N.bit_length() - 1
    unit = 8 * N
    RA = -(-(6 * W + 10) // unit) * unit
    RB = -(-(3 * W + 2) // unit) * unit
    R = RA + RB
    order, same, end, flag = sort_info(adjacency, nb + 4)
    corder, csame, cend, cflag = sort_info(coarse_adj, 3 * nc)
    parts = {"adj": adjacency.reshape(-1), "boundary": boundary.reshape(-1), "count": counts, "cadj": coarse_adj.reshape(-1),
             "order": order, "same": same, "end": end, "flag": flag, "corder": corder, "csame": csame, "cend": cend, "cflag": cflag}
    off, at = {}, 0
    for name, value in parts.items():
        off[name] = at
        at += value.shape[0]
    meta = jnp.concatenate(list(parts.values()))
    vm = pl.BlockSpec(memory_space=pltpu.VMEM)
    blk = lambda m: pltpu.VMEM((m, W, W), F32)
    b16 = lambda *s: pltpu.VMEM(s, BF16)
    f32 = lambda *s: pltpu.VMEM(s, F32)
    sd = lambda *s: jax.ShapeDtypeStruct(s, F32)
    carried, sums = pl.pallas_call(
        functools.partial(kernel, N, nb, nc, K, KC, RA, RB, off),
        out_shape=(sd(nb, W, W), sd(R, W)),
        in_specs=[pl.BlockSpec(memory_space=pltpu.SMEM)] + [vm] * 11,
        out_specs=(vm,) * 2,
        scratch_shapes=[
            blk(nb), blk(nb), blk(nb), blk(nc), blk(nc), blk(nb), blk(nb + 4),
            blk(nb * K), blk(nb * K), blk(nc * KC), blk(nb), blk(nb), blk(nc), blk(nb * K), blk(nb * K), blk(nb), blk(nc),
            b16(3 * ncd, n), b16(2 * W, n), b16(3, 512, 256), b16(3, 256, 256), b16(3, 256, 256), b16(3, 256, 256), b16(3, 256, 256),
            blk(3), blk(3), f32(W, W), f32(W, W), f32(8, 4, W, W), f32(8, 4, W, W), f32(2, 2, 8, ncd), f32(2, 2, 8, ncd),
            f32(8, n), f32(8, W), f32(8, n), f32(R, W), f32(R, W), f32(R, W),
            pltpu.SemaphoreType.DMA((8, 2)), pltpu.SemaphoreType.DMA((8, 2)), pltpu.SemaphoreType.DMA((2, 2)), pltpu.SemaphoreType.DMA((2, 2)),
            pltpu.SemaphoreType.DMA((4 * steps,)), pltpu.SemaphoreType.DMA((4 * steps,)),
        ],
        compiler_params=pltpu.CompilerParams(collective_id=0, has_side_effects=True, vmem_limit_bytes=56 * 1024 * 1024),
    )(meta, nodes.reshape(nb, W, W), edges, assign.reshape(1, n), coarse_edges, targets, ws, wr, wu, we, bias, wo)
    outs = pl.pallas_call(
        functools.partial(finish, nb, N, RA),
        out_shape=(sd(nb, W, W), sd(3, W, W), sd(3, W, W), sd(3, W, W), sd(3, W), sd(3, W), sd(4, W), sd(1, W)),
        in_specs=[vm] * 2,
        out_specs=(vm,) * 8,
    )(carried, sums)
    return (outs[7][0, :1], outs[0].reshape(n, W)) + outs[1:7]


def solution(mesh):
    both = ("groups", "dom")
    in_specs = (
        P(both, None), P(both, None, None), P(both, None), P(both, None), P(both), P(both, None), P(both, None, None), P(both),
        P(None, both), P(), P(), P(), P(), P(), P(),
    )
    out_specs = (
        P("groups"), P(both, None), P("groups", None, None), P("groups", None, None), P("groups", None, None),
        P("groups", None), P("groups", None), P("groups", None),
    )
    return jax.shard_map(functools.partial(local, mesh.shape["dom"]), mesh=mesh, in_specs=in_specs, out_specs=out_specs, check_vma=False)
```

```python
import functools

import jax
import jax.numpy as jnp
from jax import lax
from jax.experimental import pallas as pl
from jax.experimental.pallas import tpu as pltpu
from jax.sharding import PartitionSpec as P

F32 = jnp.float32
BF16 = jnp.bfloat16
W = 128


def split(x):
    hi = x.astype(BF16)
    lo = (x - hi.astype(F32)).astype(BF16)
    return hi, lo


def stacked(x):
    return jnp.concatenate(split(x), axis=0)


def doubled(w):
    hi, lo = split(w)
    return jnp.concatenate([jnp.concatenate([hi, hi], 1), jnp.concatenate([lo, lo], 1)], 0)


def dot(a, b):
    return lax.dot_general(a, b, (((1,), (0,)), ((), ())), preferred_element_type=F32)


def dot_t(a, b):
    return lax.dot_general(a, b, (((1,), (1,)), ((), ())), preferred_element_type=F32)


def halves(r):
    m = r.shape[0] // 2
    return r[:m] + r[m:]


def quads(r):
    r = halves(r)
    return r[:, :W] + r[:, W:]


def group(ref, i, g):
    return jnp.concatenate([ref[g * i + j] for j in range(g)], axis=1) if g > 1 else ref[i]


def cols(x, j):
    return x[:, j * W:(j + 1) * W]


def kernel(N, nb, nc, K, KC, RA, RB, off,
           meta, nodes, edges, assign, cedges, targets, ws, wr, wu, we, bias, wo,
           dn, res_o,
           h0, h1, h2, c0, c1, own, recv, D0, D1, D2, agg0, agg1, agg2, G, S, gr, gc,
           oh, h2s, WF, WU, WUb, WSb, WRb, WE, BI, eacc, bacc, xb, st, xs, sts, t8, w8, gp, acc, rsb, res,
           ssem, rsem, sssem, srsem, assem, arsem):
    me = lax.axis_index("dom")
    steps = N.bit_length() - 1
    n = nb * W
    ncd = nc * W
    up_ok = me < N - 1
    down_ok = me > 0

    def partner(s):
        bit = 1 << s
        return me + bit * (1 - 2 * ((me // bit) % 2))

    def dev(d):
        return {"dom": d}

    MESH = pl.DeviceIdType.MESH

    @pl.when(me == 0)
    def _():
        for x in range(8):
            xb[x, 0:2] = jnp.zeros((2, W, W), F32)
        for x in range(2):
            xs[x, 0] = jnp.zeros(xs.shape[2:], F32)

    @pl.when(me == N - 1)
    def _():
        for x in range(8):
            xb[x, 2:4] = jnp.zeros((2, W, W), F32)
        for x in range(2):
            xs[x, 1] = jnp.zeros(xs.shape[2:], F32)

    barrier = pltpu.get_barrier_semaphore()
    for d in [lax.rem(me + 1, N), lax.rem(me + N - 1, N)] + [partner(s) for s in range(steps)]:
        pl.semaphore_signal(barrier, inc=1, device_id=dev(d), device_id_type=MESH)

    def copy_to(x, small, side):
        buf, stage, a, b = (xs, sts, sssem, srsem) if small else (xb, st, ssem, rsem)
        at = side if small else pl.ds(2 * side, 2)
        return pltpu.make_async_remote_copy(
            stage.at[x, at], buf.at[x, at], a.at[x, side], b.at[x, side],
            device_id=dev(me + 1 - 2 * side), device_id_type=MESH)

    def start(x, small=False):
        @pl.when(up_ok)
        def _():
            copy_to(x, small, 0).start()

        @pl.when(down_ok)
        def _():
            copy_to(x, small, 1).start()

    def wait(x, small=False):
        @pl.when(up_ok)
        def _():
            copy_to(x, small, 0).wait_send()
            copy_to(x, small, 1).wait_recv()

        @pl.when(down_ok)
        def _():
            copy_to(x, small, 1).wait_send()
            copy_to(x, small, 0).wait_recv()

    count = meta[off["count"]]

    def live(b):
        return jnp.where(b < count, 1.0, 0.0).astype(F32)

    def one(b):
        return None

    def by(m, v):
        return v if m is None else v * m

    def tr(b, _):
        h0[b] = nodes[b].T
        return 0

    lax.fori_loop(0, nb, tr, 0)

    def stage_boundary(x, h):
        for j in range(2):
            st[x, j] = h[meta[off["boundary"] + j]]
            st[x, 2 + j] = h[meta[off["boundary"] + 2 + j]]

    stage_boundary(0, h0)
    pl.semaphore_wait(barrier, 2 + steps)
    start(0)

    def prep(l, _):
        WF[l, 0:256] = doubled(ws[l].T * 0.5)
        WF[l, 256:512] = doubled(wr[l].T * 0.5)
        WU[l] = doubled(wu[l].T)
        WUb[l] = doubled(wu[l])
        WSb[l] = doubled(ws[l])
        WRb[l] = doubled(wr[l])
        return 0

    lax.fori_loop(0, 3, prep, 0)
    for l in range(3):
        WE[l] = jnp.broadcast_to(we[l:l + 1, :] * 0.5, (W, W)).T
        BI[l] = jnp.broadcast_to(bias[l:l + 1, :] * 0.5, (W, W)).T
    acc[...] = jnp.zeros_like(acc)

    def project(l, nblk, h):
        g = min(4, nblk)

        def body(i, _):
            r = dot(WF[l], stacked(group(h, i, g)))
            o, v = halves(r[:256]), halves(r[256:])
            for j in range(g):
                own[g * i + j] = cols(o, j) + BI[l]
                recv[g * i + j] = cols(v, j)
            return 0

        lax.fori_loop(0, nblk // g, body, 0, unroll=True)

    def messages(l, nblk, k_, h, hn, D, agg, x, adj, ed, mask):
        v = halves(dot(WF[l, 256:512], stacked(group(xb.at[x], 0, 4))))
        for j in range(4):
            recv[nblk + j] = cols(v, j)

        def body(i, _):
            sums = []
            for j in range(2):
                b = 2 * i + j
                o = own[b]
                a = None
                for k in range(k_):
                    q = o + recv[meta[adj + b * k_ + k]] + WE[l] * ed[b, pl.ds(k, 1), :]
                    t = jnp.tanh(q)
                    qt = q * t
                    D[b * k_ + k] = (0.5 + 0.5 * t) * ((1.0 + q) - qt)
                    a = q + qt if a is None else a + (q + qt)
                agg[b] = a
                sums.append(a)
            u = halves(dot(WU[l], stacked(jnp.concatenate(sums, 1))))
            for j in range(2):
                b = 2 * i + j
                hn[b] = h[b] + by(mask(b), cols(u, j))
            return 0

        lax.fori_loop(0, nblk // 2, body, 0, unroll=2)

    base_of = {0: RA, 1: 0, 2: 3 * W}
    ge_of = {0: RA + 3 * W, 1: 6 * W, 2: 6 * W + 1}
    gb_of = {0: RA + 3 * W + 1, 1: 6 * W + 2, 2: 6 * W + 3}

    def add_acc(row, value):
        acc[row:row + W] += value

    def backward(l, nblk, k_, h, go, D, agg, x, y, pre, ed, mask, hook=None):
        base = base_of[l]
        hook = hook or (lambda: None)
        eacc[...] = jnp.zeros_like(eacc)
        bacc[...] = jnp.zeros_like(bacc)

        def body(i, _):
            bs = [2 * i, 2 * i + 1]
            us = stacked(jnp.concatenate([by(mask(b), go[b]) for b in bs], 1))
            ga = halves(dot(WUb[l], us))
            add_acc(base + 2 * W, quads(dot_t(stacked(group(agg, i, 2)), us)))
            sums = []
            for j, b in enumerate(bs):
                gj = cols(ga, j)
                s = e = None
                for k in range(k_):
                    m = gj * D[b * k_ + k]
                    G[b * k_ + k] = m
                    w = m * ed[b, pl.ds(k, 1), :]
                    s = m if s is None else s + m
                    e = w if e is None else e + w
                eacc[...] += e
                bacc[...] += s
                sums.append(s)
            ss = stacked(jnp.concatenate(sums, 1))
            add_acc(base, quads(dot_t(stacked(group(h, i, 2)), ss)))
            f = halves(dot(WSb[l], ss))
            for j, b in enumerate(bs):
                go[b] = go[b] + cols(f, j)
            return 0

        hook()
        pairs = nblk // 2
        lax.fori_loop(0, pairs // 2, body, 0, unroll=2)
        hook()
        lax.fori_loop(pairs // 2, pairs, body, 0, unroll=2)
        hook()
        acc[ge_of[l]:ge_of[l] + 1] = jnp.sum(eacc[...].T, axis=0, keepdims=True)
        acc[gb_of[l]:gb_of[l] + 1] = jnp.sum(bacc[...].T, axis=0, keepdims=True)

        def scan(j, run):
            run = run * meta[off[pre + "same"] + j].astype(F32) + G[meta[off[pre + "order"] + j]]
            S[j] = run
            return run

        half = nblk * k_ // 2
        run = lax.fori_loop(0, half, scan, jnp.zeros((W, W), F32), unroll=8)
        hook()
        lax.fori_loop(half, nblk * k_, scan, run, unroll=8)
        hook()

        def ext(e):
            return S[meta[off[pre + "end"] + e]] * meta[off[pre + "flag"] + e].astype(F32)

        xsx = stacked(jnp.concatenate([ext(nblk + j) for j in range(4)], 1))
        v = halves(dot(WRb[l], xsx))
        for j in range(2):
            st[y, 2 + j] = cols(v, j)
            st[y, j] = cols(v, 2 + j)
        start(y)
        hook()
        add_acc(base + W, quads(dot_t(stacked(group(xb.at[x], 0, 4)), xsx)))
        g = min(4, nblk)

        def rest(i, _):
            es = stacked(jnp.concatenate([ext(g * i + j) for j in range(g)], 1))
            f = halves(dot(WRb[l], es))
            for j in range(g):
                go[g * i + j] = go[g * i + j] + cols(f, j)
            add_acc(base + W, quads(dot_t(stacked(group(h, i, g)), es)))
            return 0

        lax.fori_loop(0, nblk // g, rest, 0, unroll=True)
        hook()
        wait(y)

    def returned(go, y, b):
        v = go[b]
        for j in range(2):
            v = v + xb[y, j] * jnp.where(meta[off["boundary"] + 2 + j] == b, 1.0, 0.0).astype(F32)
            v = v + xb[y, 2 + j] * jnp.where(meta[off["boundary"] + j] == b, 1.0, 0.0).astype(F32)
        return v

    project(0, nb, h0)

    def onehot(i, _):
        rows = lax.broadcasted_iota(jnp.int32, (W, n), 0) + i * W
        oh[pl.ds(pl.multiple_of(i * W, W), W), :] = jnp.where(rows == assign[...], 1.0, 0.0).astype(BF16)
        return 0

    lax.fori_loop(0, 3 * nc, onehot, 0)
    wait(0)
    messages(0, nb, K, h0, h1, D0, agg0, 0, off["adj"], edges, live)
    stage_boundary(1, h1)
    start(1)
    project(1, nb, h1)
    wait(1)
    messages(1, nb, K, h1, h2, D1, agg1, 1, off["adj"], edges, live)

    for b in range(nb):
        h2s[:, b * W:(b + 1) * W] = stacked(h2[b])

    def restricted(c):
        return halves(dot_t(h2s[...], oh[c * ncd:(c + 1) * ncd, :]))

    v = restricted(1)
    for j in range(nc):
        st[2, 2 + j] = cols(v, j)
    v = restricted(2)
    for j in range(nc):
        st[2, j] = cols(v, j)
    start(2)
    v = restricted(0)
    w8[...] = jnp.zeros_like(w8)
    w8[0:4] = wo[...]
    t8[...] = jnp.zeros_like(t8)
    t8[0:4] = targets[...]
    whi, wlo = split(w8[...])
    whi, wlo = whi.astype(F32), wlo.astype(F32)
    wd = jnp.concatenate([jnp.concatenate([whi, whi], 1), jnp.concatenate([wlo, wlo], 1)], 0).astype(BF16)
    fill = jnp.zeros((W - 16, W), F32)
    wt = jnp.concatenate([jnp.concatenate([whi, whi, fill], 0).T, jnp.concatenate([wlo, wlo, fill], 0).T], 0).astype(BF16)

    def rows16(x):
        hi, lo = split(x)
        return jnp.concatenate([hi.astype(F32), lo.astype(F32)], 0)

    wait(2)
    for j in range(nc):
        c0[j] = (cols(v, j) + xb[2, j] + xb[2, 2 + j]) * 0.125
        st[3, j] = c0[j]
        st[3, 2 + j] = c0[j]
    start(3)
    project(2, nc, c0)
    wait(3)
    messages(2, nc, KC, c0, c1, D2, agg2, 3, off["cadj"], cedges, one)

    c1s = stacked(group(c1, 0, nc))
    pc = halves(dot(wd, c1s))
    sts[0, 0] = pc
    sts[0, 1] = pc
    start(0, True)
    pred = halves(dot(wd, h2s[...])) + halves(dot(rows16(pc).astype(BF16), oh[0:ncd, :]))
    wait(0, True)
    pn = jnp.concatenate([rows16(xs[0, 0]), rows16(xs[0, 1])], 1).astype(BF16)
    pred = pred + halves(dot(pn, oh[ncd:3 * ncd, :]))
    err = jnp.where(lax.broadcasted_iota(jnp.int32, (8, n), 1) < count * W, pred - t8[...], 0.0)
    small = 6 * W
    e2 = err * err
    tot = e2[:, :W]
    for b in range(1, nb):
        tot = tot + cols(e2, b)
    acc[small + 8:small + 9] = jnp.broadcast_to(jnp.sum(tot).reshape(1, 1), (1, W))
    acc[small + 9:small + 10] = jnp.broadcast_to(count.astype(F32), (1, W))
    gp[...] = err * (2.0 / (4.0 * W * nb * N))
    g16 = rows16(gp[...])
    g16b = g16.astype(BF16)
    gq = halves(dot_t(g16b, oh[ncd:3 * ncd, :]))
    sts[1, 1] = gq[:, :ncd]
    sts[1, 0] = gq[:, ncd:]
    start(1, True)
    gq = halves(dot_t(g16b, oh[0:ncd, :]))
    go8 = quads(dot_t(g16b, h2s[...]))
    wait(1, True)
    gq = gq + xs[1, 0] + xs[1, 1]
    q16 = rows16(gq)
    go8 = go8 + quads(dot_t(q16.astype(BF16), c1s))
    acc[small + 4:small + 8] = go8[0:4]
    f = halves(dot(wt, jnp.concatenate([q16, jnp.zeros((W - 16, ncd), F32)], 0).astype(BF16)))
    for j in range(nc):
        gc[j] = cols(f, j)

    backward(2, nc, KC, c0, gc, D2, agg2, 3, 4, "c", cedges, one)
    for j in range(nc):
        v = (gc[j] + xb[4, j] + xb[4, 2 + j]) * 0.125
        st[5, j] = v
        st[5, 2 + j] = v
    start(5)
    gp128 = jnp.concatenate([g16, jnp.zeros((W - 16, n), F32)], 0).astype(BF16)
    f = halves(dot(wt, gp128))
    f = f + halves(dot(stacked(jnp.concatenate([st[5, j] for j in range(nc)], 1)), oh[0:ncd, :]))
    wait(5)
    f = f + halves(dot(stacked(group(xb.at[5], 0, 4)), oh[ncd:3 * ncd, :]))
    for b in range(nb):
        gr[b] = cols(f, b)

    backward(1, nb, K, h1, gr, D1, agg1, 1, 6, "", edges, live)

    def ret(b, _):
        gr[b] = returned(gr, 6, b)
        return 0

    lax.fori_loop(0, nb, ret, 0)

    def summed(base, rows, q):
        lo, size, spot = base + 0 * me, rows, base
        for s in range(steps):
            size //= 2
            mine = (me // (1 << s)) % 2
            copy = pltpu.make_async_remote_copy(
                acc.at[pl.ds(pl.multiple_of(lo + (1 - mine) * size, 8), size)], rsb.at[pl.ds(spot, size)],
                assem.at[q + s], arsem.at[q + s], device_id=dev(partner(s)), device_id_type=MESH)
            copy.start()
            yield
            copy.wait()
            lo = lo + mine * size
            keep = pl.ds(pl.multiple_of(lo, 8), size)
            acc[keep] += rsb[pl.ds(spot, size)]
            spot += size
        res[keep] = acc[keep]
        for s in range(steps - 1, -1, -1):
            mine = (me // (1 << s)) % 2
            part = res.at[pl.ds(pl.multiple_of(lo, 8), size)]
            copy = pltpu.make_async_remote_copy(
                part, part, assem.at[q + steps + s], arsem.at[q + steps + s], device_id=dev(partner(s)), device_id_type=MESH)
            copy.start()
            yield
            copy.wait()
            lo = lo - mine * size
            size *= 2

    early = summed(0, RA, 0)
    calls = iter(range(99))
    backward(0, nb, K, h0, gr, D0, agg0, 0, 7, "", edges, live, lambda: next(early, None) if next(calls) in (0, 2, 6) else None)
    late = summed(RA, RB, 2 * steps)
    next(late)

    def fin(b, _):
        dn[b] = returned(gr, 7, b).T
        return 0

    lax.fori_loop(0, nb, fin, 0)
    for _ in range(2 * steps):
        next(late, None)
        next(early, None)
    res_o[...] = res[...]


def finish(nb, N, RA, gr, res, dn, gs_o, gr_o, gu_o, ge_o, gb_o, go_o, loss_o):
    small = 6 * W
    total = res[small + 9:small + 10]
    ratio = (1.0 * nb * N) / total
    for l, base in ((0, RA), (1, 0), (2, 3 * W)):
        gs_o[l] = res[base:base + W] * ratio
        gr_o[l] = res[base + W:base + 2 * W] * ratio
        gu_o[l] = res[base + 2 * W:base + 3 * W] * ratio
    ge_o[0:1] = res[RA + 3 * W:RA + 3 * W + 1] * ratio
    ge_o[1:3] = res[small:small + 2] * ratio
    gb_o[0:1] = res[RA + 3 * W + 1:RA + 3 * W + 2] * ratio
    gb_o[1:3] = res[small + 2:small + 4] * ratio
    go_o[...] = res[small + 4:small + 8] * ratio
    loss_o[...] = res[small + 8:small + 9] / (4.0 * W * total)

    def out(b, _):
        dn[b] = gr[b] * ratio
        return 0

    lax.fori_loop(0, nb, out, 0)


def sort_info(adj, ext):
    a = adj.reshape(-1)
    m = a.shape[0]
    i = jnp.arange(m, dtype=jnp.int32)
    rank = jnp.sum(((a[None, :] < a[:, None]) | ((a[None, :] == a[:, None]) & (i[None, :] < i[:, None]))).astype(jnp.int32), 1)
    hit = rank[None, :] == i[:, None]
    order = jnp.sum(jnp.where(hit, i[None, :], 0), 1)
    value = jnp.sum(jnp.where(hit, a[None, :], 0), 1)
    before = jnp.sum(jnp.where(rank[None, :] == i[:, None] - 1, a[None, :], 0), 1)
    same = ((value == before) & (i > 0)).astype(jnp.int32)
    e = jnp.arange(ext, dtype=jnp.int32)
    end = jnp.maximum(jnp.sum((a[None, :] <= e[:, None]).astype(jnp.int32), 1) - 1, 0)
    flag = (jnp.sum((a[None, :] == e[:, None]).astype(jnp.int32), 1) > 0).astype(jnp.int32)
    return order, same, end, flag


def local(N, nodes, edges, adjacency, boundary, assign, coarse_adj, coarse_edges, counts, targets, ws, wr, wu, we, bias, wo):
    nb, K, _ = edges.shape
    nc, KC, _ = coarse_edges.shape
    n = nb * W
    ncd = nc * W
    steps = N.bit_length() - 1
    unit = 8 * N
    RA = -(-(6 * W + 10) // unit) * unit
    RB = -(-(3 * W + 2) // unit) * unit
    R = RA + RB
    order, same, end, flag = sort_info(adjacency, nb + 4)
    corder, csame, cend, cflag = sort_info(coarse_adj, 3 * nc)
    parts = {"adj": adjacency.reshape(-1), "boundary": boundary.reshape(-1), "count": counts, "cadj": coarse_adj.reshape(-1),
             "order": order, "same": same, "end": end, "flag": flag, "corder": corder, "csame": csame, "cend": cend, "cflag": cflag}
    off, at = {}, 0
    for name, value in parts.items():
        off[name] = at
        at += value.shape[0]
    meta = jnp.concatenate(list(parts.values()))
    vm = pl.BlockSpec(memory_space=pltpu.VMEM)
    blk = lambda m: pltpu.VMEM((m, W, W), F32)
    b16 = lambda *s: pltpu.VMEM(s, BF16)
    f32 = lambda *s: pltpu.VMEM(s, F32)
    sd = lambda *s: jax.ShapeDtypeStruct(s, F32)
    carried, sums = pl.pallas_call(
        functools.partial(kernel, N, nb, nc, K, KC, RA, RB, off),
        out_shape=(sd(nb, W, W), sd(R, W)),
        in_specs=[pl.BlockSpec(memory_space=pltpu.SMEM)] + [vm] * 11,
        out_specs=(vm,) * 2,
        scratch_shapes=[
            blk(nb), blk(nb), blk(nb), blk(nc), blk(nc), blk(nb), blk(nb + 4),
            blk(nb * K), blk(nb * K), blk(nc * KC), blk(nb), blk(nb), blk(nc), blk(nb * K), blk(nb * K), blk(nb), blk(nc),
            b16(3 * ncd, n), b16(2 * W, n), b16(3, 512, 256), b16(3, 256, 256), b16(3, 256, 256), b16(3, 256, 256), b16(3, 256, 256),
            blk(3), blk(3), f32(W, W), f32(W, W), f32(8, 4, W, W), f32(8, 4, W, W), f32(2, 2, 8, ncd), f32(2, 2, 8, ncd),
            f32(8, n), f32(8, W), f32(8, n), f32(R, W), f32(R, W), f32(R, W),
            pltpu.SemaphoreType.DMA((8, 2)), pltpu.SemaphoreType.DMA((8, 2)), pltpu.SemaphoreType.DMA((2, 2)), pltpu.SemaphoreType.DMA((2, 2)),
            pltpu.SemaphoreType.DMA((4 * steps,)), pltpu.SemaphoreType.DMA((4 * steps,)),
        ],
        compiler_params=pltpu.CompilerParams(collective_id=0, has_side_effects=True, vmem_limit_bytes=56 * 1024 * 1024),
    )(meta, nodes.reshape(nb, W, W), edges, assign.reshape(1, n), coarse_edges, targets, ws, wr, wu, we, bias, wo)
    outs = pl.pallas_call(
        functools.partial(finish, nb, N, RA),
        out_shape=(sd(nb, W, W), sd(3, W, W), sd(3, W, W), sd(3, W, W), sd(3, W), sd(3, W), sd(4, W), sd(1, W)),
        in_specs=[vm] * 2,
        out_specs=(vm,) * 8,
    )(carried, sums)
    return (outs[7][0, :1], outs[0].reshape(n, W)) + outs[1:7]


def solution(mesh):
    both = ("groups", "dom")
    in_specs = (
        P(both, None), P(both, None, None), P(both, None), P(both, None), P(both), P(both, None), P(both, None, None), P(both),
        P(None, both), P(), P(), P(), P(), P(), P(),
    )
    out_specs = (
        P("groups"), P(both, None), P("groups", None, None), P("groups", None, None), P("groups", None, None),
        P("groups", None), P("groups", None), P("groups", None),
    )
    return jax.shard_map(functools.partial(local, mesh.shape["dom"]), mesh=mesh, in_specs=in_specs, out_specs=out_specs, check_vma=False)
```
